32 devices in a mesh: seq: 32 (over z, y, x, core), wt: 1.
Axes of the slice: x: 2, y: 2, z: 4, core: 2. Of those that a mesh axis runs over, the one named last changes fastest.
Arguments:
- hidden_rows: bfloat16 [8192, 2688], P('seq'), may hold values from -6 to 6
- value_weight: bfloat16 [2688, 1536], P('seq', 'wt'), may hold values from -0.125 to 0.125
- queries: bfloat16 [8192, 3072], P('seq', 'wt'), may hold values from -60 to 60
- key_rows: bfloat16 [8192, 1536], P('seq', 'wt'), may hold values from -4.1 to 4.1
- out_grad: bfloat16 [8192, 3072], P('seq', 'wt'), may hold values from -6 to 6
- segments: int32 [8192], replicated, may hold values from 0 to 3, never falling along the last dimension, each value on 1 to 4096 neighbouring positions
Outputs:
- attention: bfloat16 [8192, 3072], P('seq', 'wt')
- weight_grad: float32 [2688, 1536], P('seq', 'wt')
The draws below stay inside these ranges and needn't reach their ends.
Inputs may be any that keep to these rules, and one draw needn't show every extreme that they name: `segments`: never falling along the slab.
All inputs are finite; a program needn't handle non-finite values.
Results may differ from the reference program's by a relative error of at most 0.0057.
Values may be sent and summed in bfloat16 or wider, within the bound.
A program may use at most 128 MiB of HBM per device.

```python
import math
import jax
import jax.numpy as jnp
import numpy as np
from jax import lax

D = 2688
H = 24
KVH = 12
HD = 128
WINDOW = 1024
TOK_DEV = 256
TOKENS = 8192
REACH = 4


def shared_draw(key):
    base = jax.random.fold_in(key, 4242)
    key_first, key_second = jax.random.split(base, 2)
    key_part = jnp.clip(jax.random.normal(key_first, (TOKENS, KVH * HD), jnp.float32), -4.0, 4.0)
    query_part = jnp.clip(jax.random.normal(key_second, (TOKENS, H * HD), jnp.float32), -4.0, 4.0)
    return (query_part, key_part)


def draw_queries(key, part):
    return shared_draw(key)[0].astype(jnp.bfloat16)


def draw_key_rows(key, part):
    return shared_draw(key)[1].astype(jnp.bfloat16)


def raised(values, own_key, source, target, parts, factor):
    owner, partner = [(jnp.arange(values.shape[position]) // (values.shape[position] // parts)).reshape([-1 if axis == position else 1 for axis in range(values.ndim)]) for position in (source, target)]
    chosen = jax.random.permutation(own_key, parts)[partner]
    strong = (owner == chosen) | (owner == (partner + parts // 2) % parts)
    return jnp.where(strong, factor * values, values)


def shard_levels(own_key, extent, pieces, least, top_value):
    def one(position, parts):
        draws = jax.random.uniform(jax.random.fold_in(jax.random.fold_in(own_key, 6), position), (parts,), jnp.float32, least / len(pieces), top_value / len(pieces))
        return jnp.repeat(jnp.exp(draws), extent[position] // parts).reshape((-1,) + (1,) * (len(extent) - position - 1))

    loudness = one(*pieces[0])
    for cut in pieces[1:]:
        loudness = loudness * one(*cut)
    return loudness


def split_up(number_of, total, bound, slope):
    portions = [(1 << 20) // math.isqrt(rank ** slope) + 1 for rank in range(2, number_of + 1)]
    surplus, counts = total - bound - (number_of - 1), [1] * (number_of - 1)
    while surplus > 0:
        movable = [i for i in range(number_of - 1) if counts[i] < bound]
        whole, left = sum([portions[i] for i in movable]), surplus
        for i in movable:
            addition = min(bound - counts[i], max(1, left * portions[i] // whole), surplus)
            counts[i] = counts[i] + addition
            surplus = surplus - addition
    return np.array([bound] + counts)


def uneven(stream_key, number_of, total, bound, skew):
    if number_of == 2:
        one = jax.random.randint(stream_key, (), max(1, total - bound), min(bound, total - 1) + 1)
        return jnp.stack([one, total - one])
    lengths = jnp.asarray(split_up(number_of, total, bound, skew), jnp.int32)
    couples = (number_of - 1) // 2
    donor, taker = lengths[1:1 + 2 * couples:2], lengths[2:2 + 2 * couples:2]
    room = jnp.minimum(donor - 1, bound - taker)
    moved = jax.random.randint(jax.random.fold_in(stream_key, 1), (couples,), 0, 1 << 20) % (room + 1)
    lengths = lengths.at[1:1 + 2 * couples:2].set(donor - moved).at[2:2 + 2 * couples:2].set(taker + moved)
    return lengths[jax.random.permutation(jax.random.fold_in(stream_key, 2), number_of)]


def centred(stream_key, dims, deviation, limit, cuts=(), kind=jnp.bfloat16):
    array = deviation * jax.random.normal(stream_key, dims, jnp.float32)
    if cuts:
        array = array * shard_levels(stream_key, dims, cuts, -0.22, 0.18)
    return jnp.clip(array, -limit, limit).astype(kind)


def heavy_noise(key, shape, width, bound, cuts, heavy, kind=jnp.bfloat16):
    drawn = width * jax.random.normal(key, shape, jnp.float32)
    if cuts:
        drawn = drawn * shard_levels(key, shape, cuts, -0.22, 0.18)
    return jnp.clip(raised(drawn, jax.random.fold_in(key, 3), *heavy), -bound, bound).astype(kind)


def setup_inputs(seed: int = 0) -> dict:
    key_list = jax.random.split(jax.random.key(seed), 7)
    return {
        "hidden_rows": heavy_noise(key_list[0], (TOKENS, D), 1.0, 6.0, ((0, 32),), (0, 1, 32, 2.75)),
        "value_weight": centred(key_list[1], (D, KVH * HD), D ** -0.5, 0.125, ((0, 32),)),
        "queries": draw_queries(jax.random.fold_in(key_list[6], 71), 0),
        "key_rows": draw_key_rows(jax.random.fold_in(key_list[6], 71), 0),
        "out_grad": centred(key_list[4], (TOKENS, H * HD), 1.0, 6.0, ((0, 32),)),
        "segments": jnp.searchsorted(jnp.cumsum(uneven(key_list[5], max(2, TOKENS // (2 * WINDOW)), TOKENS, min(4 * WINDOW, TOKENS // 2), 0)), jnp.arange(TOKENS), side="right").astype(jnp.int32),
    }


def reference(hidden_rows, value_weight, queries, key_rows, out_grad, segments):
    rows_here = TOK_DEV
    blocks_back = REACH
    key_span = (blocks_back + 1) * rows_here
    padding = blocks_back * rows_here
    group_size = H // KVH
    kv_width = KVH * HD
    scale = 1.0 / math.sqrt(HD)
    values = jnp.dot(hidden_rows, value_weight, preferred_element_type=jnp.float32).astype(jnp.bfloat16)
    keys_padded = jnp.concatenate([jnp.zeros((padding, kv_width), jnp.bfloat16), key_rows], axis=0)
    values_padded = jnp.concatenate([jnp.zeros((padding, kv_width), jnp.bfloat16), values], axis=0)
    segs_padded = jnp.concatenate([jnp.full((padding,), -1, jnp.int32), segments.astype(jnp.int32)], axis=0)
    distance = jnp.arange(rows_here, dtype=jnp.int32)[:, None] + padding - jnp.arange(key_span, dtype=jnp.int32)[None, :]

    def one_block(carried, block_index):
        anchor = (block_index * rows_here).astype(jnp.int32)
        query_four = lax.dynamic_slice_in_dim(queries, anchor, rows_here, 0).reshape(rows_here, KVH, group_size, HD).astype(jnp.float32)
        grad_four = lax.dynamic_slice_in_dim(out_grad, anchor, rows_here, 0).reshape(rows_here, KVH, group_size, HD).astype(jnp.float32)
        key_three = lax.dynamic_slice_in_dim(keys_padded, anchor, key_span, 0).reshape(key_span, KVH, HD).astype(jnp.float32)
        value_three = lax.dynamic_slice_in_dim(values_padded, anchor, key_span, 0).reshape(key_span, KVH, HD).astype(jnp.float32)
        query_seg = lax.dynamic_slice_in_dim(segments.astype(jnp.int32), anchor, rows_here, 0)
        key_seg = lax.dynamic_slice_in_dim(segs_padded, anchor, key_span, 0)
        allowed = (distance >= 0) & (distance < WINDOW) & (query_seg[:, None] == key_seg[None, :])
        scores = jnp.einsum('tkgd,lkd->kgtl', query_four, key_three) * scale
        scores = jnp.where(allowed[None, None], scores, -1e+30)
        highest = lax.optimization_barrier(jnp.max(scores, axis=-1, keepdims=True))
        weights = jnp.exp(scores - highest)
        probs = (weights / lax.optimization_barrier(jnp.sum(weights, axis=-1, keepdims=True))).astype(jnp.bfloat16)
        probs_wide = probs.astype(jnp.float32)
        output = jnp.einsum('kgtl,lkd->tkgd', probs_wide, value_three).reshape(rows_here, H * HD).astype(jnp.bfloat16)
        partial_value = jnp.einsum('kgtl,tkgd->lkd', probs_wide, grad_four).reshape(key_span, kv_width).astype(jnp.bfloat16)
        current = lax.dynamic_slice_in_dim(carried, anchor, key_span, 0)
        carried = lax.dynamic_update_slice_in_dim(carried, current + partial_value.astype(jnp.float32), anchor, 0)
        return (carried, output)
    initial = jnp.zeros((padding + TOKENS, kv_width), jnp.float32)
    summed, outputs = lax.scan(one_block, initial, jnp.arange(TOKENS // rows_here, dtype=jnp.int32))
    attention = outputs.reshape(TOKENS, H * HD)
    value_grad = summed[padding:].astype(jnp.bfloat16)
    weight_grad = jnp.dot(hidden_rows.T, value_grad, preferred_element_type=jnp.float32)
    return (attention, weight_grad)
```

```python
import math

import jax
import jax.numpy as jnp
from jax import lax
from jax.sharding import PartitionSpec as P

HD = 128
WINDOW = 1024
GROUP = 8


def passed_along(block, axis, distance):
    devices = range(lax.axis_size(axis))
    route = [(i - distance, i) for i in devices if i - distance in devices]
    return lax.ppermute(block, axis, route)


def attend(query_four, grad_four, key_three, value_three, allowed, scale):
    scores = (
        jnp.einsum("tkgd,lkd->kgtl", query_four, key_three, preferred_element_type=jnp.float32)
        * scale
    )
    scores = jnp.where(allowed[None, None], scores, -1e30)
    highest = jnp.max(scores, axis=-1, keepdims=True)
    weights = jnp.exp(scores - highest)
    probs = (weights / jnp.sum(weights, axis=-1, keepdims=True)).astype(jnp.bfloat16)
    output = jnp.einsum("kgtl,lkd->tkgd", probs, value_three, preferred_element_type=jnp.float32)
    partial_value = jnp.einsum(
        "kgtl,tkgd->lkd", probs, grad_four, preferred_element_type=jnp.float32
    )
    return (output, partial_value)


def group_of(devices):
    return math.gcd(devices, GROUP)


def within_group(block, step):
    devices = lax.axis_size("seq")
    return lax.ppermute(block, "seq", [(i, i ^ step) for i in range(devices)])


def hidden_exchange(hidden_rows):
    devices = lax.axis_size("seq")
    group = group_of(devices)
    rank = lax.rem(lax.axis_index("seq"), group)
    tokens, features = hidden_rows.shape
    columns = hidden_rows.T.reshape(devices // group, group, features // devices, tokens)
    received = []
    for step in range(group):
        block = lax.dynamic_index_in_dim(columns, rank ^ step, 1, keepdims=False)
        received.append(within_group(block, step) if step else block)
    return jnp.concatenate(received, axis=-1)


def weight_gradient(hidden_sent, value_grad):
    devices = lax.axis_size("seq")
    group = group_of(devices)
    groups = devices // group
    received = [value_grad] + [within_group(value_grad, step) for step in range(1, group)]
    terms = lax.dot_general(
        hidden_sent,
        jnp.concatenate(received, axis=0),
        (((2,), (0,)), ((), ())),
        preferred_element_type=jnp.float32,
    )
    here = lax.axis_index("seq") // group
    total = lax.dynamic_index_in_dim(terms, here, 0, keepdims=False)
    rounded = terms.astype(jnp.bfloat16)
    for step in range(1, groups):
        block = lax.dynamic_index_in_dim(rounded, lax.rem(here + step, groups), 0, keepdims=False)
        route = [(i, (i + step * group) % devices) for i in range(devices)]
        total = total + lax.ppermute(block, "seq", route).astype(jnp.float32)
    return total


def per_device(hidden_rows, value_weight, queries, key_rows, out_grad, segments):
    rows_here = hidden_rows.shape[0]
    kv_width = value_weight.shape[1]
    kv_heads = kv_width // HD
    group_size = queries.shape[1] // kv_width
    blocks_back = (WINDOW + rows_here - 2) // rows_here
    key_span = (blocks_back + 1) * rows_here
    padding = blocks_back * rows_here
    scale = 1.0 / math.sqrt(HD)
    hidden_sent = hidden_exchange(hidden_rows)
    values = jnp.dot(
        hidden_rows,
        lax.all_gather(value_weight, "seq", axis=0, tiled=True),
        preferred_element_type=jnp.float32,
    ).astype(jnp.bfloat16)
    earlier = [passed_along((key_rows, values), "seq", offset + 1) for offset in range(blocks_back)]
    ordered = list(reversed(earlier))
    key_window = jnp.concatenate([member[0] for member in ordered] + [key_rows], axis=0)
    value_window = jnp.concatenate([member[1] for member in ordered] + [values], axis=0)
    position = lax.axis_index("seq")
    segs_padded = jnp.concatenate([jnp.full((padding,), -1, jnp.int32), segments], axis=0)
    key_seg = lax.dynamic_slice_in_dim(segs_padded, position * rows_here, key_span, 0)
    query_seg = lax.dynamic_slice_in_dim(segments, position * rows_here, rows_here, 0)
    distance = (
        jnp.arange(rows_here, dtype=jnp.int32)[:, None]
        + padding
        - jnp.arange(key_span, dtype=jnp.int32)[None, :]
    )
    allowed = (distance >= 0) & (distance < WINDOW) & (query_seg[:, None] == key_seg[None, :])
    query_four = queries.reshape(rows_here, kv_heads, group_size, HD)
    grad_four = out_grad.reshape(rows_here, kv_heads, group_size, HD)
    key_three = key_window.reshape(key_span, kv_heads, HD)
    value_three = value_window.reshape(key_span, kv_heads, HD)
    output, partial_value = attend(query_four, grad_four, key_three, value_three, allowed, scale)
    attention = output.reshape(rows_here, kv_width * group_size).astype(jnp.bfloat16)
    partial_value = partial_value.reshape(key_span, kv_width).astype(jnp.bfloat16)
    gathered = partial_value[padding:].astype(jnp.float32)
    for offset in range(1, blocks_back + 1):
        portion = partial_value[
            (blocks_back - offset) * rows_here : (blocks_back - offset + 1) * rows_here
        ]
        gathered = gathered + passed_along(portion, "seq", -offset).astype(jnp.float32)
    value_grad = gathered.astype(jnp.bfloat16)
    weight_grad = weight_gradient(hidden_sent, value_grad)
    return (attention, weight_grad)


def solution(mesh):
    in_specs = (P("seq", None), P("seq", "wt"), P("seq", "wt"), P("seq", "wt"), P("seq", "wt"), P())
    out_specs = (P("seq", "wt"), P("seq", "wt"))
    return jax.shard_map(
        per_device, mesh=mesh, in_specs=in_specs, out_specs=out_specs, check_vma=False
    )
```

```python
import math

import jax
import jax.numpy as jnp
from jax import lax
from jax.sharding import PartitionSpec as P

HD = 128
WINDOW = 1024
GROUP = 8


def passed_along(block, axis, distance):
    devices = range(lax.axis_size(axis))
    route = [(i - distance, i) for i in devices if i - distance in devices]
    return lax.ppermute(block, axis, route)


def within_group(block, step):
    devices = lax.axis_size("seq")
    return lax.ppermute(block, "seq", [(i, i ^ step) for i in range(devices)])


def window_of(block, pairs, odd):
    rows = block.shape[0]
    straight = [block] + [passed_along(block, "seq", 2 * k) for k in range(1, pairs + 1)]
    wanted = lax.dynamic_slice_in_dim(
        jnp.concatenate(straight, axis=0), odd * rows, pairs * rows, 0
    )
    swapped = within_group(wanted, 1)
    ordered = [block]
    for k in range(pairs):
        ordered = [straight[k + 1], swapped[k * rows : (k + 1) * rows]] + ordered
    return jnp.concatenate(ordered, axis=0)


def summed_back(partial_value, pairs, odd, rows):
    def term(distance):
        start = (2 * pairs - distance) * rows
        return partial_value[start : start + rows]

    swapped = within_group(
        jnp.concatenate([term(2 * k + 1) for k in range(pairs)], axis=0), 1
    ).astype(jnp.float32)
    zero = jnp.zeros((rows, partial_value.shape[1]), jnp.float32)
    pieces = [swapped[k * rows : (k + 1) * rows] for k in range(pairs)]
    sums = [
        term(2 * k).astype(jnp.float32) + jnp.where(odd == 1, before, after)
        for k, (before, after) in enumerate(zip([zero] + pieces, pieces + [zero]))
    ]
    total = sums[0]
    for k in range(1, pairs + 1):
        portion = sums[k].astype(jnp.bfloat16)
        total = total + passed_along(portion, "seq", -2 * k).astype(jnp.float32)
    return total.astype(jnp.bfloat16)


def attend(query_four, grad_four, key_three, allowed, scale):
    scores = (
        jnp.einsum("tkgd,lkd->kgtl", query_four, key_three, preferred_element_type=jnp.float32)
        * scale
    )
    scores = jnp.where(allowed[None, None], scores, -1e30)
    highest = jnp.max(scores, axis=-1, keepdims=True)
    weights = jnp.exp(scores - highest)
    probs = (weights / jnp.sum(weights, axis=-1, keepdims=True)).astype(jnp.bfloat16)
    partial_value = jnp.einsum(
        "kgtl,tkgd->lkd", probs, grad_four, preferred_element_type=jnp.float32
    )
    return (probs, partial_value)


def group_of(devices):
    return math.gcd(devices, GROUP)


def hidden_exchange(hidden_rows):
    devices = lax.axis_size("seq")
    group = group_of(devices)
    rank = lax.rem(lax.axis_index("seq"), group)
    tokens, features = hidden_rows.shape
    columns = hidden_rows.T.reshape(devices // group, group, features // devices, tokens)
    received = []
    for step in list(range(0, group, 2)) + list(range(1, group, 2)):
        block = lax.dynamic_index_in_dim(columns, rank ^ step, 1, keepdims=False)
        received.append(within_group(block, step) if step else block)
    return jnp.concatenate(received, axis=-1)


def weight_gradient(hidden_sent, value_grad):
    devices = lax.axis_size("seq")
    group = group_of(devices)
    groups = devices // group
    received = [value_grad] + [within_group(value_grad, step) for step in range(2, group, 2)]
    received = jnp.concatenate(received, axis=0)
    terms = jnp.zeros((), jnp.float32)
    half = received.shape[0]
    for start, block in ((0, received), (half, within_group(received, 1))):
        terms = terms + lax.dot_general(
            hidden_sent[:, :, start : start + half],
            block,
            (((2,), (0,)), ((), ())),
            preferred_element_type=jnp.float32,
        )
    here = lax.axis_index("seq") // group
    total = lax.dynamic_index_in_dim(terms, here, 0, keepdims=False)
    rounded = terms.astype(jnp.bfloat16)
    for step in range(1, groups):
        block = lax.dynamic_index_in_dim(rounded, lax.rem(here + step, groups), 0, keepdims=False)
        route = [(i, (i + step * group) % devices) for i in range(devices)]
        total = total + lax.ppermute(block, "seq", route).astype(jnp.float32)
    return total


def per_device(hidden_rows, value_weight, queries, key_rows, out_grad, segments):
    rows_here = hidden_rows.shape[0]
    kv_width = value_weight.shape[1]
    kv_heads = kv_width // HD
    group_size = queries.shape[1] // kv_width
    blocks_back = (WINDOW + rows_here - 2) // rows_here
    key_span = (blocks_back + 1) * rows_here
    padding = blocks_back * rows_here
    scale = 1.0 / math.sqrt(HD)
    values = jnp.dot(
        hidden_rows,
        lax.all_gather(value_weight, "seq", axis=0, tiled=True),
        preferred_element_type=jnp.float32,
    ).astype(jnp.bfloat16)
    pairs = blocks_back // 2
    odd = lax.rem(lax.axis_index("seq"), 2)
    key_window = window_of(key_rows, pairs, odd)
    key_window, hidden_later = lax.optimization_barrier((key_window, hidden_rows))
    hidden_sent = hidden_exchange(hidden_later)
    position = lax.axis_index("seq")
    segs_padded = jnp.concatenate([jnp.full((padding,), -1, jnp.int32), segments], axis=0)
    key_seg = lax.dynamic_slice_in_dim(segs_padded, position * rows_here, key_span, 0)
    query_seg = lax.dynamic_slice_in_dim(segments, position * rows_here, rows_here, 0)
    distance = (
        jnp.arange(rows_here, dtype=jnp.int32)[:, None]
        + padding
        - jnp.arange(key_span, dtype=jnp.int32)[None, :]
    )
    allowed = (distance >= 0) & (distance < WINDOW) & (query_seg[:, None] == key_seg[None, :])
    query_four = queries.reshape(rows_here, kv_heads, group_size, HD)
    grad_four = out_grad.reshape(rows_here, kv_heads, group_size, HD)
    key_three = key_window.reshape(key_span, kv_heads, HD)
    probs, partial_value = attend(query_four, grad_four, key_three, allowed, scale)
    partial_value = partial_value.reshape(key_span, kv_width).astype(jnp.bfloat16)
    value_grad = summed_back(partial_value, pairs, odd, rows_here)
    value_grad, values = lax.optimization_barrier((value_grad, values))
    weight_grad = weight_gradient(hidden_sent, value_grad)
    value_three = window_of(values, pairs, odd).reshape(key_span, kv_heads, HD)
    output = jnp.einsum("kgtl,lkd->tkgd", probs, value_three, preferred_element_type=jnp.float32)
    attention = output.reshape(rows_here, kv_width * group_size).astype(jnp.bfloat16)
    return (attention, weight_grad)


def solution(mesh):
    in_specs = (P("seq", None), P("seq", "wt"), P("seq", "wt"), P("seq", "wt"), P("seq", "wt"), P())
    out_specs = (P("seq", "wt"), P("seq", "wt"))
    return jax.shard_map(
        per_device, mesh=mesh, in_specs=in_specs, out_specs=out_specs, check_vma=False
    )
```

```python
import math

import jax
import jax.numpy as jnp
from jax import lax
from jax.sharding import PartitionSpec as P

HD = 128
WINDOW = 1024
GROUP = 8


def passed_along(block, axis, distance):
    devices = range(lax.axis_size(axis))
    route = [(i - distance, i) for i in devices if i - distance in devices]
    return lax.ppermute(block, axis, route)


def within_group(block, step):
    devices = lax.axis_size("seq")
    return lax.ppermute(block, "seq", [(i, i ^ step) for i in range(devices)])


def window_of(block, pairs, odd, beside=None):
    rows = block.shape[0]
    straight = [block] + [passed_along(block, "seq", 2 * k) for k in range(1, pairs + 1)]
    if beside is not None:
        straight, beside = lax.optimization_barrier((straight, beside))
        block = straight[0]
    wanted = lax.dynamic_slice_in_dim(
        jnp.concatenate(straight, axis=0), odd * rows, pairs * rows, 0
    )
    swapped = within_group(wanted, 1)
    ordered = [block]
    for k in range(pairs):
        ordered = [straight[k + 1], swapped[k * rows : (k + 1) * rows]] + ordered
    return jnp.concatenate(ordered, axis=0), beside


def summed_back(partial_value, values, pairs, odd, rows):
    def term(distance):
        start = (2 * pairs - distance) * rows
        return partial_value[start : start + rows]

    swapped = within_group(
        jnp.concatenate([term(2 * k + 1) for k in range(pairs)], axis=0), 1
    ).astype(jnp.float32)
    zero = jnp.zeros((rows, partial_value.shape[1]), jnp.float32)
    pieces = [swapped[k * rows : (k + 1) * rows] for k in range(pairs)]
    sums = [
        term(2 * k).astype(jnp.float32) + jnp.where(odd == 1, before, after)
        for k, (before, after) in enumerate(zip([zero] + pieces, pieces + [zero]))
    ]
    total = sums[0]
    for k in range(1, pairs + 1):
        portion = sums[k].astype(jnp.bfloat16)
        total = total + passed_along(portion, "seq", -2 * k).astype(jnp.float32)
        if k == 1:
            total, values = lax.optimization_barrier((total, values))
    return total.astype(jnp.bfloat16), values


def attend(query_four, grad_four, key_three, allowed, scale):
    scores = (
        jnp.einsum("tkgd,lkd->kgtl", query_four, key_three, preferred_element_type=jnp.float32)
        * scale
    )
    scores = jnp.where(allowed[None, None], scores, -1e30)
    highest = jnp.max(scores, axis=-1, keepdims=True)
    weights = jnp.exp(scores - highest)
    probs = (weights / jnp.sum(weights, axis=-1, keepdims=True)).astype(jnp.bfloat16)
    partial_value = jnp.einsum(
        "kgtl,tkgd->lkd", probs, grad_four, preferred_element_type=jnp.float32
    )
    return (probs, partial_value)


def group_of(devices):
    return math.gcd(devices, GROUP)


def hidden_exchange(hidden_rows):
    devices = lax.axis_size("seq")
    group = group_of(devices)
    rank = lax.rem(lax.axis_index("seq"), group)
    tokens, features = hidden_rows.shape
    columns = hidden_rows.T.reshape(devices // group, group, features // devices, tokens)
    received = []
    for step in list(range(0, group, 2)) + list(range(1, group, 2)):
        block = lax.dynamic_index_in_dim(columns, rank ^ step, 1, keepdims=False)
        received.append(within_group(block, step) if step else block)
    return jnp.concatenate(received, axis=-1)


def weight_gradient(hidden_sent, value_grad, values, pairs, odd):
    devices = lax.axis_size("seq")
    group = group_of(devices)
    groups = devices // group
    received = [value_grad] + [within_group(value_grad, step) for step in range(2, group, 2)]
    received, values = lax.optimization_barrier((jnp.concatenate(received, axis=0), values))
    terms = jnp.zeros((), jnp.float32)
    half = received.shape[0]
    for start, block in ((0, received), (half, within_group(received, 1))):
        terms = terms + lax.dot_general(
            hidden_sent[:, :, start : start + half],
            block,
            (((2,), (0,)), ((), ())),
            preferred_element_type=jnp.float32,
        )
    value_window, terms = window_of(values, pairs, odd, terms)
    here = lax.axis_index("seq") // group
    total = lax.dynamic_index_in_dim(terms, here, 0, keepdims=False)
    rounded = terms.astype(jnp.bfloat16)
    others = []
    for step in range(1, groups):
        block = lax.dynamic_index_in_dim(rounded, lax.rem(here + step, groups), 0, keepdims=False)
        route = [(i, (i + step * group) % devices) for i in range(devices)]
        others.append(lax.ppermute(block, "seq", route))
    return total, others, value_window


def per_device(hidden_rows, value_weight, queries, key_rows, out_grad, segments):
    rows_here = hidden_rows.shape[0]
    kv_width = value_weight.shape[1]
    kv_heads = kv_width // HD
    group_size = queries.shape[1] // kv_width
    blocks_back = (WINDOW + rows_here - 2) // rows_here
    key_span = (blocks_back + 1) * rows_here
    padding = blocks_back * rows_here
    scale = 1.0 / math.sqrt(HD)
    features = value_weight.shape[0]
    extra = -features % 16
    weight_padded = lax.all_gather(
        jnp.pad(value_weight, ((0, extra), (0, 0))), "seq", axis=0, tiled=True
    )
    pairs = blocks_back // 2
    odd = lax.rem(lax.axis_index("seq"), 2)
    key_window, _ = window_of(key_rows, pairs, odd)
    hidden_padded = jnp.pad(
        hidden_rows.reshape(rows_here, -1, features), ((0, 0), (0, 0), (0, extra))
    ).reshape(rows_here, -1)
    key_window, hidden_later = lax.optimization_barrier((key_window, hidden_rows))
    hidden_sent = hidden_exchange(hidden_later)
    position = lax.axis_index("seq")
    segs_padded = jnp.concatenate([jnp.full((padding,), -1, jnp.int32), segments], axis=0)
    key_seg = lax.dynamic_slice_in_dim(segs_padded, position * rows_here, key_span, 0)
    query_seg = lax.dynamic_slice_in_dim(segments, position * rows_here, rows_here, 0)
    distance = (
        jnp.arange(rows_here, dtype=jnp.int32)[:, None]
        + padding
        - jnp.arange(key_span, dtype=jnp.int32)[None, :]
    )
    allowed = (distance >= 0) & (distance < WINDOW) & (query_seg[:, None] == key_seg[None, :])
    query_four = queries.reshape(rows_here, kv_heads, group_size, HD)
    grad_four = out_grad.reshape(rows_here, kv_heads, group_size, HD)
    key_three = key_window.reshape(key_span, kv_heads, HD)
    probs, partial_value = attend(query_four, grad_four, key_three, allowed, scale)
    partial_value = partial_value.reshape(key_span, kv_width).astype(jnp.bfloat16)
    partial_value, hidden_sent, hidden_padded = lax.optimization_barrier(
        (partial_value, hidden_sent, hidden_padded)
    )
    values = jnp.dot(hidden_padded, weight_padded, preferred_element_type=jnp.float32)
    value_grad, values = summed_back(
        partial_value, values.astype(jnp.bfloat16), pairs, odd, rows_here
    )
    weight_grad, others, value_window = weight_gradient(hidden_sent, value_grad, values, pairs, odd)
    value_three = value_window.reshape(key_span, kv_heads, HD)
    output = jnp.einsum("kgtl,lkd->tkgd", probs, value_three, preferred_element_type=jnp.float32)
    attention = output.reshape(rows_here, kv_width * group_size).astype(jnp.bfloat16)
    weight_grad, attention = lax.optimization_barrier((weight_grad, attention))
    for block in others:
        weight_grad = weight_grad + block.astype(jnp.float32)
    return (attention, weight_grad)


def solution(mesh):
    in_specs = (P("seq", None), P("seq", "wt"), P("seq", "wt"), P("seq", "wt"), P("seq", "wt"), P())
    out_specs = (P("seq", "wt"), P("seq", "wt"))
    return jax.shard_map(
        per_device, mesh=mesh, in_specs=in_specs, out_specs=out_specs, check_vma=False
    )
```
